32 devices in a mesh: grp: 16 (over z, y, core), mem: 2 (over x).
Axes of the slice: x: 2, y: 2, z: 4, core: 2. Of those that a mesh axis runs over, the one named last changes fastest.
Arguments:
- features: bfloat16 [16384, 256], P(('grp', 'mem')), may hold values from -6 to 6
- initial: bfloat16 [16384, 256], P(('grp', 'mem')), may hold values from -6 to 6
- weight: bfloat16 [256, 256], replicated, may hold values from -0.375 to 0.375
- mask_in: int32 [16384, 512], P(('grp', 'mem')), may hold values 0 or 1
- mask_out: int32 [16384, 512], P(('grp', 'mem')), may hold values 0 or 1
- history: bfloat16 [32768, 256], P(('grp', 'mem')), may hold values from -6 to 6
- serve_rows: int32 [16384], P(('grp', 'mem')), may hold values from 0 to 1023, as said below
- push_rows: int32 [16384], P(('grp', 'mem')), may hold values from 0 to 1023, as said below
- cotangent: bfloat16 [16384, 256], P(('grp', 'mem')), may hold values from -6 to 6
Outputs:
- grad_weight: float32 [256, 256], replicated
- new_history: bfloat16 [32768, 256], P(('grp', 'mem'))
The draws below stay inside these ranges and needn't reach their ends.
Inputs may be any that keep to these rules, and one draw needn't show every extreme that they name: `serve_rows`: the 512 entries of one partition are distinct local rows. `push_rows`: the 512 entries of one partition are distinct local rows.
All inputs are finite; a program needn't handle non-finite values. No bound on the sum of `mask_in` or of `mask_out` on one device may be relied on, other than what follows from the above.
Results may differ from the reference program's by a relative error of at most 0.005.
Values may be sent and summed in bfloat16 or wider, within the bound.
A program may use at most 64 MiB of HBM per device.

```python
import jax
import jax.numpy as jnp
from jax import lax

D = 256
BATCH = 512
PULL = 512
HROWS = 1024
TOKENS = 16384
SERVED = 16384
TABLE = 32768
N_GRP = 16
N_MEM = 2


def distinct_rows(key, blocks, count):

    def one_block(sub):
        first, second = jax.random.split(sub)
        base = jax.random.permutation(first, HROWS - 1)[:count - 1].astype(jnp.int32)
        full = jnp.concatenate([base, jnp.full((1,), HROWS - 1, jnp.int32)])
        return full[jax.random.permutation(second, count)]
    return jax.vmap(one_block)(jax.random.split(key, blocks)).reshape(-1)


def draw_serve_rows(key, part):
    key = jax.random.fold_in(key, 11)
    return distinct_rows(key, SERVED // PULL, PULL)


def draw_push_rows(key, part):
    key = jax.random.fold_in(key, 23)
    return distinct_rows(key, TOKENS // BATCH, BATCH)


def place_ends(result, own_key, least, top_value):
    dims = result.shape
    index_at = [jax.random.randint(jax.random.fold_in(own_key, axis), (), 0, dims[axis]) for axis in range(len(dims))]
    result = result.at[tuple(index_at)].set(least)
    longest = dims.index(max(dims))
    index_at[longest] = (index_at[longest] + 1) % dims[longest]
    return result.at[tuple(index_at)].set(top_value)


def steps_of(own_key, shape, shards, low, high):
    def one(axis_at, shards_of):
        heights = jax.random.uniform(jax.random.fold_in(jax.random.fold_in(own_key, 6), axis_at), (shards_of,), jnp.float32, low / len(shards), high / len(shards))
        return jnp.repeat(jnp.exp(heights), shape[axis_at] // shards_of).reshape((-1,) + (1,) * (len(shape) - axis_at - 1))

    gain = one(*shards[0])
    for cut in shards[1:]:
        gain = gain * one(*cut)
    return gain


def normal_values(key, shape, width, bound, pieces=(), dtype=jnp.bfloat16):
    loudness = steps_of(key, shape, pieces, -0.22, 0.18) if pieces else 1.0
    array = jax.random.normal(key, shape, jnp.float32) * width * loudness
    return jnp.minimum(jnp.maximum(array, -bound), bound).astype(dtype)


def setup_inputs(seed: int = 0) -> dict:
    key_of = jax.random.split(jax.random.key(seed), 10)
    return {
        "features": normal_values(key_of[0], (TOKENS, D), 1.0, 6.0, ((0, 32),)),
        "initial": normal_values(key_of[1], (TOKENS, D), 1.0, 6.0, ((0, 32),)),
        "weight": normal_values(key_of[2], (D, D), D ** -0.5, 0.375),
        "mask_in": place_ends((jax.random.randint(key_of[3], (TOKENS, BATCH), 0, 8) < 1).astype(jnp.int32), jax.random.fold_in(key_of[3], 1), 0, 1),
        "mask_out": place_ends((jax.random.randint(key_of[4], (TOKENS, PULL), 0, 8) < 1).astype(jnp.int32), jax.random.fold_in(key_of[4], 1), 0, 1),
        "history": normal_values(key_of[5], (TABLE, D), 1.0, 6.0, ((0, 32),)),
        "serve_rows": draw_serve_rows(jax.random.fold_in(key_of[9], 71), 0),
        "push_rows": draw_push_rows(jax.random.fold_in(key_of[9], 71), 0),
        "cotangent": normal_values(key_of[8], (TOKENS, D), 1.0, 6.0, ((0, 32),)),
    }


ALPHA = 0.1
BETA = 0.5

def layer_rows(features, initial, weight, mask_in, mask_out, pulled, cotangent):
    degree = 1.0 + lax.optimization_barrier(jnp.sum(mask_in, axis=1)).astype(jnp.float32) + lax.optimization_barrier(jnp.sum(mask_out, axis=1)).astype(jnp.float32)
    summed = features.astype(jnp.float32)
    summed = summed + jnp.dot(mask_in.astype(jnp.bfloat16), features, preferred_element_type=jnp.float32)
    summed = summed + jnp.dot(mask_out.astype(jnp.bfloat16), pulled, preferred_element_type=jnp.float32)
    summed = summed / degree[:, None]
    support = ((1.0 - ALPHA) * summed + ALPHA * initial.astype(jnp.float32)).astype(jnp.bfloat16)
    mixed = (1.0 - BETA) * support.astype(jnp.float32) + BETA * jnp.dot(support, weight, preferred_element_type=jnp.float32)
    sigma = jax.nn.sigmoid(mixed)
    embedded = (mixed * sigma).astype(jnp.bfloat16)
    delta = (cotangent.astype(jnp.float32) * sigma * (1.0 + mixed * (1.0 - sigma))).astype(jnp.bfloat16)
    partial_grad = lax.dot_general(support, delta, (((0,), (0,)), ((), ())), preferred_element_type=jnp.float32)
    return (embedded, partial_grad)

def reference(features, initial, weight, mask_in, mask_out, history, serve_rows, push_rows, cotangent):
    devices = N_GRP * N_MEM
    per_owner = PULL // N_MEM
    per_dest = BATCH // N_MEM
    hist_four = history.reshape(N_GRP, N_MEM, HROWS, D)
    serve_three = serve_rows.reshape(N_GRP, N_MEM, PULL)
    picked = jax.vmap(jax.vmap(lambda table, rows: table[rows]))(hist_four, serve_three)
    picked = picked.reshape(N_GRP, N_MEM, N_MEM, per_owner, D).transpose(0, 2, 1, 3, 4).reshape(devices, PULL, D)

    def step(total, items):
        emb_rows, partial_grad = layer_rows(items[0], items[1], weight, items[2], items[3], items[4], items[5])
        return (total + partial_grad, emb_rows)
    stacked = (features.reshape(devices, BATCH, D), initial.reshape(devices, BATCH, D), mask_in.reshape(devices, BATCH, BATCH), mask_out.reshape(devices, BATCH, PULL), picked, cotangent.reshape(devices, BATCH, D))
    total, embedded = lax.scan(step, jnp.zeros((D, D), jnp.float32), stacked)
    grad_weight = total * (BETA / jnp.sqrt(jnp.float32(TOKENS)))
    moved = embedded.reshape(N_GRP, N_MEM, N_MEM, per_dest, D).transpose(0, 2, 1, 3, 4).reshape(devices, BATCH, D)
    tables = history.reshape(devices, HROWS, D)
    targets = push_rows.reshape(devices, BATCH)
    new_history = jax.vmap(lambda table, rows, values: table.at[rows].set(values))(tables, targets, moved)
    return (grad_weight, new_history.reshape(TABLE, D))
```

```python
import functools
import math

import jax
import jax.numpy as jnp
from jax import lax
from jax.experimental import pallas as pl
from jax.experimental.pallas import tpu as pltpu
from jax.sharding import PartitionSpec as P

ALPHA = 0.1
BETA = 0.5
F32 = jnp.float32
BF16 = jnp.bfloat16
MESH = pl.DeviceIdType.MESH


def dot(a, b, contract=((1,), (0,))):
    return lax.dot_general(a, b, (contract, ((), ())), preferred_element_type=F32)


def kernel(
    groups,
    members,
    low,
    factor,
    features_in,
    initial_in,
    weight_in,
    mask_in_in,
    mask_out_in,
    history_in,
    serve_in,
    push_in,
    cotangent_in,
    grad_out,
    history_out,
    features,
    initial,
    weight,
    mask_in,
    mask_out,
    history,
    serve,
    push,
    cotangent,
    served,
    pulled,
    embedded,
    pushed,
    base,
    table,
    part,
    parts,
    chunk,
    chunks,
    final,
    finals,
    total,
    load_sem,
    store_sem,
    pull_send,
    pull_recv,
    push_send,
    push_recv,
    part_send,
    part_recv,
    chunk_send,
    chunk_recv,
    final_send,
    final_recv,
):
    g = lax.axis_index("grp")
    m = lax.axis_index("mem")
    batch, width = features.shape
    pull = serve.shape[1]
    rows = history.shape[0]
    k = pull // members
    q = batch // members
    plane = low * members
    planes = groups // low
    high = g // low
    inner = g % low
    spot = inner * members + m
    depth = width // plane

    def at_spot(p):
        return (high * low + p // members, p % members)

    def at_plane(h):
        return (h * low + inner, m)

    barrier = pltpu.get_barrier_semaphore()
    for off in range(1, plane):
        pl.semaphore_signal(
            barrier, inc=1, device_id=at_spot((spot + off) % plane), device_id_type=MESH
        )
    for off in range(1, planes):
        pl.semaphore_signal(
            barrier, inc=1, device_id=at_plane((high + off) % planes), device_id_type=MESH
        )

    loads = {}
    for i, (name, src, dst) in enumerate(
        (
            ("serve", serve_in, serve),
            ("history", history_in, history),
            ("push", push_in, push),
            ("features", features_in, features),
            ("mask_in", mask_in_in, mask_in),
            ("mask_out", mask_out_in, mask_out),
            ("initial", initial_in, initial),
            ("weight", weight_in, weight),
            ("cotangent", cotangent_in, cotangent),
        )
    ):
        loads[name] = pltpu.make_async_copy(src, dst, load_sem.at[i])
        loads[name].start()

    loads["serve"].wait()
    loads["history"].wait()

    def gather(j):
        wanted = serve[:, pl.ds(pl.multiple_of(j * k, 128), k)]
        wanted = jnp.transpose(jnp.broadcast_to(wanted, (128, k)))
        lane = lax.broadcasted_iota(jnp.int32, (k, 128), 1)
        found = dot(
            jnp.concatenate(
                [
                    jnp.where(wanted == lane + 128 * i, 1.0, 0.0).astype(BF16)
                    for i in range(rows // 128)
                ],
                axis=1,
            ),
            history[...],
        )
        return found.astype(BF16)

    for off in range(1, members):
        j = (m + off) % members
        served[off - 1] = gather(j)

    pl.semaphore_wait(barrier, plane - 1 + planes - 1)
    pulls = []
    for off in range(1, members):
        j = (m + off) % members
        copy = pltpu.make_async_remote_copy(
            src_ref=served.at[off - 1],
            dst_ref=pulled.at[off - 1],
            send_sem=pull_send.at[off - 1],
            recv_sem=pull_recv.at[off - 1],
            device_id=(g, j),
            device_id_type=MESH,
        )
        copy.start()
        pulls.append(copy)

    own = gather(m)
    loads["features"].wait()
    loads["mask_in"].wait()
    loads["mask_out"].wait()
    summed = features[...].astype(F32) + dot(
        mask_in[...].astype(F32).astype(BF16), features[...]
    )
    degree = 1.0 + jnp.sum(
        (mask_in[...] + mask_out[...]).astype(F32), axis=1, keepdims=True
    )
    inverse = 1.0 / degree

    def columns(j):
        return (
            mask_out[:, pl.ds(pl.multiple_of(j * k, 128), k)].astype(F32).astype(BF16)
        )

    summed = summed + dot(columns(m), own)

    loads["push"].wait()
    loads["initial"].wait()
    loads["weight"].wait()
    loads["cotangent"].wait()

    def hot(j):
        targets = push[:, pl.ds(pl.multiple_of(j * q, 128), q)]
        row = lax.broadcasted_iota(jnp.int32, (rows, q), 0)
        return jnp.where(row == targets, 1.0, 0.0).astype(BF16)

    row = lax.broadcasted_iota(jnp.int32, (rows, batch), 0)
    marks = jnp.where(row == push[...], 1.0, 0.0).astype(BF16)
    covered = dot(marks, jnp.ones((batch, 128), BF16))
    covered = jnp.concatenate([covered] * (width // 128), axis=1)
    base[...] = jnp.where(covered > 0.5, 0.0, history[...].astype(F32))

    for off in range(1, members):
        j = (m - off + members) % members
        pulls[off - 1].wait_recv()
        summed = summed + dot(columns(j), pulled[off - 1])

    support = (
        (1.0 - ALPHA) * (summed * inverse) + ALPHA * initial[...].astype(F32)
    ).astype(BF16)
    mixed = (1.0 - BETA) * support.astype(F32) + BETA * dot(support, weight[...])
    sigma = jax.nn.sigmoid(mixed)
    embedded[...] = (mixed * sigma).astype(BF16)
    delta = (
        cotangent[...].astype(F32) * sigma * (1.0 + mixed * (1.0 - sigma))
    ).astype(BF16)
    partial = factor * dot(support, delta, ((0,), (0,)))
    part[...] = partial.astype(part.dtype)

    sends = []
    for off in range(1, plane):
        p = (spot + off) % plane
        copy = pltpu.make_async_remote_copy(
            src_ref=part.at[pl.ds(pl.multiple_of(p * depth, depth), depth)],
            dst_ref=parts.at[off - 1],
            send_sem=part_send.at[off - 1],
            recv_sem=part_recv.at[off - 1],
            device_id=at_spot(p),
            device_id_type=MESH,
        )
        copy.start()
        sends.append(copy)

    pushes = []
    for off in range(1, members):
        j = (m + off) % members
        copy = pltpu.make_async_remote_copy(
            src_ref=embedded.at[pl.ds(pl.multiple_of(j * q, q), q)],
            dst_ref=pushed.at[off - 1],
            send_sem=push_send.at[off - 1],
            recv_sem=push_recv.at[off - 1],
            device_id=(g, j),
            device_id_type=MESH,
        )
        copy.start()
        pushes.append(copy)

    base[...] += dot(hot(m), embedded[pl.ds(pl.multiple_of(m * q, q), q), :])

    mine = part[pl.ds(pl.multiple_of(spot * depth, depth), depth), :].astype(F32)
    for off in range(1, plane):
        sends[off - 1].wait_recv()
        mine = mine + parts[off - 1].astype(F32)
    chunk[...] = mine.astype(chunk.dtype)
    chunks[high] = chunk[...]
    rounds = []
    for off in range(1, planes):
        h = (high + off) % planes
        copy = pltpu.make_async_remote_copy(
            src_ref=chunk,
            dst_ref=chunks.at[high],
            send_sem=chunk_send.at[off - 1],
            recv_sem=chunk_recv.at[off - 1],
            device_id=at_plane(h),
            device_id_type=MESH,
        )
        copy.start()
        rounds.append(copy)

    fresh = base[...]
    for off in range(1, members):
        j = (m - off + members) % members
        pushes[off - 1].wait_recv()
        fresh = fresh + dot(hot(j), pushed[off - 1])
    table[...] = fresh.astype(BF16)
    store = pltpu.make_async_copy(table, history_out, store_sem.at[0])
    store.start()

    for copy in rounds:
        copy.wait_recv()
    whole = chunks[0].astype(F32)
    for h in range(1, planes):
        whole = whole + chunks[h].astype(F32)
    final[...] = whole.astype(final.dtype)
    finals[spot] = final[...]
    lasts = []
    for off in range(1, plane):
        p = (spot + off) % plane
        copy = pltpu.make_async_remote_copy(
            src_ref=final,
            dst_ref=finals.at[spot],
            send_sem=final_send.at[off - 1],
            recv_sem=final_recv.at[off - 1],
            device_id=at_spot(p),
            device_id_type=MESH,
        )
        copy.start()
        lasts.append(copy)
    for copy in lasts:
        copy.wait_recv()
    total[...] = finals[...].astype(F32).reshape(width, width)
    write = pltpu.make_async_copy(total, grad_out, store_sem.at[1])
    write.start()
    for copy in pulls + sends + pushes + rounds + lasts:
        copy.wait_send()
    store.wait()
    write.wait()


def local(
    groups,
    members,
    features,
    initial,
    weight,
    mask_in,
    mask_out,
    history,
    serve_rows,
    push_rows,
    cotangent,
):
    batch, width = features.shape
    pull = serve_rows.shape[0]
    rows = history.shape[0]
    low = max(1, 8 // members)
    while groups % low:
        low -= 1
    plane = low * members
    planes = groups // low
    depth = width // plane
    wire = BF16
    factor = BETA / math.sqrt(groups * members * batch)
    vmem = pltpu.VMEM
    dma = pltpu.SemaphoreType.DMA
    anywhere = pl.BlockSpec(memory_space=pl.ANY)
    return pl.pallas_call(
        functools.partial(kernel, groups, members, low, factor),
        out_shape=(
            jax.ShapeDtypeStruct((width, width), F32),
            jax.ShapeDtypeStruct((rows, width), BF16),
        ),
        in_specs=[anywhere] * 9,
        out_specs=(anywhere, anywhere),
        scratch_shapes=[
            vmem(features.shape, BF16),
            vmem(initial.shape, BF16),
            vmem(weight.shape, BF16),
            vmem(mask_in.shape, jnp.int32),
            vmem(mask_out.shape, jnp.int32),
            vmem(history.shape, BF16),
            vmem((1, pull), jnp.int32),
            vmem((1, batch), jnp.int32),
            vmem(cotangent.shape, BF16),
            vmem((members - 1, pull // members, width), BF16),
            vmem((members - 1, pull // members, width), BF16),
            vmem((batch, width), BF16),
            vmem((members - 1, batch // members, width), BF16),
            vmem((rows, width), F32),
            vmem((rows, width), BF16),
            vmem((width, width), wire),
            vmem((plane - 1, depth, width), wire),
            vmem((depth, width), wire),
            vmem((planes, depth, width), wire),
            vmem((depth, width), wire),
            vmem((plane, depth, width), wire),
            vmem((width, width), F32),
            dma((9,)),
            dma((2,)),
            dma((members - 1,)),
            dma((members - 1,)),
            dma((members - 1,)),
            dma((members - 1,)),
            dma((plane - 1,)),
            dma((plane - 1,)),
            dma((planes - 1,)),
            dma((planes - 1,)),
            dma((plane - 1,)),
            dma((plane - 1,)),
        ],
        compiler_params=pltpu.CompilerParams(
            collective_id=0, has_side_effects=True, vmem_limit_bytes=60 * 1024 * 1024
        ),
    )(
        features,
        initial,
        weight,
        mask_in,
        mask_out,
        history,
        serve_rows.reshape(1, pull),
        push_rows.reshape(1, batch),
        cotangent,
    )


def solution(mesh):
    groups = mesh.shape["grp"]
    members = mesh.shape["mem"]
    split = P(("grp", "mem"), None)
    return jax.shard_map(
        functools.partial(local, groups, members),
        mesh=mesh,
        in_specs=(split, split, P(), split, split, split, P(("grp", "mem")), P(("grp", "mem")), split),
        out_specs=(P(), split),
        check_vma=False,
    )
```

```python
import functools
import math

import jax
import jax.numpy as jnp
from jax import lax
from jax.experimental import pallas as pl
from jax.experimental.pallas import tpu as pltpu
from jax.sharding import PartitionSpec as P

ALPHA = 0.1
BETA = 0.5
BLOCK = 256
F32 = jnp.float32
BF16 = jnp.bfloat16
MESH = pl.DeviceIdType.MESH


def dot(a, b, contract=((1,), (0,))):
    return lax.dot_general(a, b, (contract, ((), ())), preferred_element_type=F32)


def kernel(
    groups,
    members,
    low,
    factor,
    features_in,
    initial_in,
    weight_in,
    mask_in_in,
    mask_out_in,
    history_in,
    serve_in,
    push_in,
    cotangent_in,
    grad_out,
    history_out,
    features,
    initial,
    weight,
    mask_in,
    mask_out,
    history,
    serve,
    push,
    cotangent,
    served,
    pulled,
    embedded,
    pushed,
    base,
    known,
    scale,
    others,
    part,
    parts,
    chunk,
    chunks,
    final,
    finals,
    load_sem,
    corner_sem,
    line_sem,
    pull_send,
    pull_recv,
    push_send,
    push_recv,
    part_send,
    part_recv,
    chunk_send,
    chunk_recv,
    final_send,
    final_recv,
):
    g = lax.axis_index("grp")
    m = lax.axis_index("mem")
    batch, width = features.shape
    pull = serve.shape[1]
    rows = history.shape[0]
    k = pull // members
    q = batch // members
    plane = low * members
    planes = groups // low
    high = g // low
    inner = g % low
    spot = inner * members + m
    depth = width // plane
    block = min(batch, BLOCK)
    blocks = [pl.ds(i, block) for i in range(0, batch, block)]

    def at_plane(h):
        return (h * low + inner, m)

    offsets = [
        (di, dm) for di in range(low) for dm in range(members) if di or dm
    ]
    offsets.sort(key=lambda o: -((o[0] > 0) + (o[1] > 0)))

    def shifted(di, dm):
        return (high * low + (inner + di) % low, (m + dm) % members)

    chained = 2 < planes <= 4
    barrier = pltpu.get_barrier_semaphore()

    def signal(semaphore, device):
        pl.semaphore_signal(semaphore, inc=1, device_id=device, device_id_type=MESH)

    near = [o for o in offsets if 0 in o]
    for di, dm in near:
        signal(barrier, shifted(di, dm))
    if chained:

        def along(semaphores):
            @pl.when(high > 0)
            def _():
                signal(semaphores[0], at_plane(high - 1))

            @pl.when(high < planes - 1)
            def _():
                signal(semaphores[1], at_plane(high + 1))

        def heard(semaphores):
            @pl.when(high < planes - 1)
            def _():
                pl.semaphore_wait(semaphores[0], 1)

            @pl.when(high > 0)
            def _():
                pl.semaphore_wait(semaphores[1], 1)

        along((barrier, barrier))
        beside = (high > 0).astype(jnp.int32) + (high < planes - 1).astype(jnp.int32)
    else:
        for off in range(1, planes):
            signal(barrier, at_plane((high + off) % planes))
        beside = planes - 1

    loads = {}
    for i, (name, src, dst) in enumerate(
        (
            ("serve", serve_in, serve),
            ("history", history_in, history),
            ("push", push_in, push),
            ("features", features_in, features),
            ("mask_in", mask_in_in, mask_in),
            ("mask_out", mask_out_in, mask_out),
            ("initial", initial_in, initial),
            ("weight", weight_in, weight),
            ("cotangent", cotangent_in, cotangent),
        )
    ):
        loads[name] = pltpu.make_async_copy(src, dst, load_sem.at[i])
        loads[name].start()

    loads["serve"].wait()
    loads["history"].wait()

    def gather(j):
        wanted = serve[:, pl.ds(pl.multiple_of(j * k, 128), k)]
        wanted = jnp.transpose(jnp.broadcast_to(wanted, (128, k)))
        lane = lax.broadcasted_iota(jnp.int32, (k, 128), 1)
        found = dot(
            jnp.concatenate(
                [
                    jnp.where(wanted == lane + 128 * i, 1.0, 0.0).astype(BF16)
                    for i in range(rows // 128)
                ],
                axis=1,
            ),
            history[...],
        )
        return found.astype(BF16)

    for off in range(1, members):
        j = (m + off) % members
        served[off - 1] = gather(j)

    pl.semaphore_wait(barrier, len(near) + beside)
    pulls = []
    for off in range(1, members):
        j = (m + off) % members
        copy = pltpu.make_async_remote_copy(
            src_ref=served.at[off - 1],
            dst_ref=pulled.at[off - 1],
            send_sem=pull_send.at[off - 1],
            recv_sem=pull_recv.at[off - 1],
            device_id=(g, j),
            device_id_type=MESH,
        )
        copy.start()
        pulls.append(copy)
    for di in range(1, low):
        signal(corner_sem, shifted(di, 0))
    if chained:
        along((line_sem.at[0, 0], line_sem.at[0, 1]))

    own = gather(m)
    loads["features"].wait()
    loads["mask_in"].wait()
    loads["mask_out"].wait()
    loads["initial"].wait()

    def columns(j, rows_at):
        return (
            mask_out[rows_at, pl.ds(pl.multiple_of(j * k, 128), k)]
            .astype(F32)
            .astype(BF16)
        )

    for at in blocks:
        summed = features[at, :].astype(F32)
        summed = summed + dot(mask_in[at, :].astype(F32).astype(BF16), features[...])
        summed = summed + dot(columns(m, at), own)
        degree = 1.0 + jnp.sum(
            (mask_in[at, :] + mask_out[at, :]).astype(F32), axis=1, keepdims=True
        )
        share = jnp.broadcast_to((1.0 - ALPHA) / degree, (block, width))
        scale[at, :] = share
        known[at, :] = share * summed + ALPHA * initial[at, :].astype(F32)
        for off in range(1, members):
            others[off - 1, at, :] = columns((m - off + members) % members, at)

    loads["weight"].wait()
    loads["cotangent"].wait()
    if chained:
        heard((line_sem.at[0, 0], line_sem.at[0, 1]))
        along((line_sem.at[1, 0], line_sem.at[1, 1]))

    for copy in pulls:
        copy.wait_recv()
    partial = None
    for at in blocks:
        extra = dot(others[0, at, :], pulled[0])
        for off in range(2, members):
            extra = extra + dot(others[off - 1, at, :], pulled[off - 1])
        support = (known[at, :] + scale[at, :] * extra).astype(BF16)
        mixed = (1.0 - BETA) * support.astype(F32) + BETA * dot(support, weight[...])
        sigma = 0.5 + 0.5 * jnp.tanh(0.5 * mixed)
        embedded[at, :] = (mixed * sigma).astype(BF16)
        delta = (
            cotangent[at, :].astype(F32) * sigma * (1.0 + mixed * (1.0 - sigma))
        ).astype(BF16)
        term = dot(support, delta, ((0,), (0,)))
        partial = term if partial is None else partial + term
    part[...] = (factor * partial).astype(part.dtype)
    if low > 1:
        pl.semaphore_wait(corner_sem, low - 1)

    sends = []
    for i, (di, dm) in enumerate(offsets):
        p = (inner + di) % low * members + (m + dm) % members
        copy = pltpu.make_async_remote_copy(
            src_ref=part.at[pl.ds(pl.multiple_of(p * depth, depth), depth)],
            dst_ref=parts.at[i],
            send_sem=part_send.at[i],
            recv_sem=part_recv.at[i],
            device_id=shifted(di, dm),
            device_id_type=MESH,
        )
        copy.start()
        sends.append(copy)

    loads["push"].wait()

    def hot(j):
        targets = push[:, pl.ds(pl.multiple_of(j * q, 128), q)]
        row = lax.broadcasted_iota(jnp.int32, (rows, q), 0)
        return jnp.where(row == targets, 1.0, 0.0).astype(BF16)

    covered = dot(hot(0), jnp.ones((q, 128), BF16))
    for j in range(1, members):
        covered = covered + dot(hot(j), jnp.ones((q, 128), BF16))
    covered = jnp.concatenate([covered] * (width // 128), axis=1)
    base[...] = jnp.where(covered > 0.5, 0.0, history[...].astype(F32)) + dot(
        hot(m), embedded[pl.ds(pl.multiple_of(m * q, q), q), :]
    )

    mine = part[pl.ds(pl.multiple_of(spot * depth, depth), depth), :].astype(F32)
    for off in range(1, plane):
        sends[off - 1].wait_recv()
        mine = mine + parts[off - 1].astype(F32)
    chunk[...] = mine.astype(chunk.dtype)
    chunks[high] = chunk[...]
    if chained:
        heard((line_sem.at[1, 0], line_sem.at[1, 1]))
    rounds = []
    for off in range(1, planes):
        h = (high + off) % planes
        copy = pltpu.make_async_remote_copy(
            src_ref=chunk,
            dst_ref=chunks.at[high],
            send_sem=chunk_send.at[off - 1],
            recv_sem=chunk_recv.at[off - 1],
            device_id=at_plane(h),
            device_id_type=MESH,
        )
        copy.start()
        rounds.append(copy)

    pushes = []
    for off in range(1, members):
        j = (m + off) % members
        copy = pltpu.make_async_remote_copy(
            src_ref=embedded.at[pl.ds(pl.multiple_of(j * q, q), q)],
            dst_ref=pushed.at[off - 1],
            send_sem=push_send.at[off - 1],
            recv_sem=push_recv.at[off - 1],
            device_id=(g, j),
            device_id_type=MESH,
        )
        copy.start()
        pushes.append(copy)

    for copy in rounds:
        copy.wait_recv()
    whole = chunks[0].astype(F32)
    for h in range(1, planes):
        whole = whole + chunks[h].astype(F32)
    final[...] = whole.astype(final.dtype)
    finals[spot] = final[...]
    lasts = []
    for i, (di, dm) in enumerate(offsets):
        copy = pltpu.make_async_remote_copy(
            src_ref=final,
            dst_ref=finals.at[spot],
            send_sem=final_send.at[i],
            recv_sem=final_recv.at[i],
            device_id=shifted(di, dm),
            device_id_type=MESH,
        )
        copy.start()
        lasts.append(copy)
    fresh = base[...]
    for off in range(1, members):
        j = (m - off + members) % members
        pushes[off - 1].wait_recv()
        fresh = fresh + dot(hot(j), pushed[off - 1])
    history_out[...] = fresh.astype(BF16)

    for copy in lasts:
        copy.wait_recv()
    grad_out[...] = finals[...].astype(F32).reshape(width, width)
    for copy in pulls + sends + pushes + rounds + lasts:
        copy.wait_send()


def local(
    groups,
    members,
    features,
    initial,
    weight,
    mask_in,
    mask_out,
    history,
    serve_rows,
    push_rows,
    cotangent,
):
    batch, width = features.shape
    pull = serve_rows.shape[0]
    rows = history.shape[0]
    low = max(1, 8 // members)
    while groups % low:
        low -= 1
    plane = low * members
    planes = groups // low
    depth = width // plane
    wire = BF16
    factor = BETA / math.sqrt(groups * members * batch)
    vmem = pltpu.VMEM
    dma = pltpu.SemaphoreType.DMA
    anywhere = pl.BlockSpec(memory_space=pl.ANY)
    return pl.pallas_call(
        functools.partial(kernel, groups, members, low, factor),
        out_shape=(
            pltpu.VMEM((width, width), F32),
            pltpu.VMEM((rows, width), BF16),
        ),
        in_specs=[anywhere] * 9,
        out_specs=(pl.BlockSpec(memory_space=pltpu.VMEM),)*2,
        scratch_shapes=[
            vmem(features.shape, BF16),
            vmem(initial.shape, BF16),
            vmem(weight.shape, BF16),
            vmem(mask_in.shape, jnp.int32),
            vmem(mask_out.shape, jnp.int32),
            vmem(history.shape, BF16),
            vmem((1, pull), jnp.int32),
            vmem((1, batch), jnp.int32),
            vmem(cotangent.shape, BF16),
            vmem((members - 1, pull // members, width), BF16),
            vmem((members - 1, pull // members, width), BF16),
            vmem((batch, width), BF16),
            vmem((members - 1, batch // members, width), BF16),
            vmem((rows, width), F32),
            vmem((batch, width), F32),
            vmem((batch, width), F32),
            vmem((members - 1, batch, pull // members), BF16),
            vmem((width, width), wire),
            vmem((plane - 1, depth, width), wire),
            vmem((depth, width), wire),
            vmem((planes, depth, width), wire),
            vmem((depth, width), wire),
            vmem((plane, depth, width), wire),
            dma((9,)),
            pltpu.SemaphoreType.REGULAR,
            pltpu.SemaphoreType.REGULAR((2, 2)),
            dma((members - 1,)),
            dma((members - 1,)),
            dma((members - 1,)),
            dma((members - 1,)),
            dma((plane - 1,)),
            dma((plane - 1,)),
            dma((planes - 1,)),
            dma((planes - 1,)),
            dma((plane - 1,)),
            dma((plane - 1,)),
        ],
        compiler_params=pltpu.CompilerParams(
            collective_id=0, has_side_effects=True, vmem_limit_bytes=62 * 1024 * 1024
        ),
    )(
        features,
        initial,
        weight,
        mask_in,
        mask_out,
        history,
        serve_rows.reshape(1, pull),
        push_rows.reshape(1, batch),
        cotangent,
    )


def solution(mesh):
    groups = mesh.shape["grp"]
    members = mesh.shape["mem"]
    split = P(("grp", "mem"), None)
    return jax.shard_map(
        functools.partial(local, groups, members),
        mesh=mesh,
        in_specs=(split, split, P(), split, split, split, P(("grp", "mem")), P(("grp", "mem")), split),
        out_specs=(P(), split),
        check_vma=False,
    )
```

```python
import functools
import math

import jax
import jax.numpy as jnp
from jax import lax
from jax.experimental import pallas as pl
from jax.experimental.pallas import tpu as pltpu
from jax.sharding import PartitionSpec as P

ALPHA = 0.1
BETA = 0.5
BLOCK = 256
F32 = jnp.float32
BF16 = jnp.bfloat16
MESH = pl.DeviceIdType.MESH


def dot(a, b, contract=((1,), (0,))):
    return lax.dot_general(a, b, (contract, ((), ())), preferred_element_type=F32)


def kernel(
    groups,
    members,
    low,
    factor,
    features_in,
    initial_in,
    weight_in,
    mask_in_in,
    mask_out_in,
    history_in,
    serve_in,
    push_in,
    cotangent_in,
    grad_out,
    history_out,
    features,
    initial,
    weight,
    mask_in,
    mask_out,
    history,
    serve,
    push,
    cotangent,
    served,
    pulled,
    embedded,
    pushed,
    base,
    known,
    scale,
    others,
    part,
    parts,
    chunk,
    chunks,
    final,
    finals,
    load_sem,
    corner_sem,
    line_sem,
    pull_send,
    pull_recv,
    push_send,
    push_recv,
    part_send,
    part_recv,
    chunk_send,
    chunk_recv,
    final_send,
    final_recv,
):
    g = lax.axis_index("grp")
    m = lax.axis_index("mem")
    batch, width = features.shape
    pull = serve.shape[1]
    rows = history.shape[0]
    k = pull // members
    q = batch // members
    plane = low * members
    planes = groups // low
    high = g // low
    inner = g % low
    spot = inner * members + m
    depth = width // plane
    block = min(batch, BLOCK)
    blocks = [pl.ds(i, block) for i in range(0, batch, block)]

    def at_plane(h):
        return (h * low + inner, m)

    offsets = [
        (di, dm) for di in range(low) for dm in range(members) if di or dm
    ]
    offsets.sort(key=lambda o: -((o[0] > 0) + (o[1] > 0)))

    def shifted(di, dm):
        return (high * low + (inner + di) % low, (m + dm) % members)

    chained = 2 < planes <= 4
    barrier = pltpu.get_barrier_semaphore()

    def signal(semaphore, device):
        pl.semaphore_signal(semaphore, inc=1, device_id=device, device_id_type=MESH)

    near = [o for o in offsets if 0 in o]
    for di, dm in near:
        signal(barrier, shifted(di, dm))
    if chained:

        def along(semaphores):
            @pl.when(high > 0)
            def _():
                signal(semaphores[0], at_plane(high - 1))

            @pl.when(high < planes - 1)
            def _():
                signal(semaphores[1], at_plane(high + 1))

        def heard(semaphores):
            @pl.when(high < planes - 1)
            def _():
                pl.semaphore_wait(semaphores[0], 1)

            @pl.when(high > 0)
            def _():
                pl.semaphore_wait(semaphores[1], 1)

        along((barrier, barrier))
        beside = (high > 0).astype(jnp.int32) + (high < planes - 1).astype(jnp.int32)
    else:
        for off in range(1, planes):
            signal(barrier, at_plane((high + off) % planes))
        beside = planes - 1

    loads = {}
    for i, (name, src, dst) in enumerate(
        (
            ("serve", serve_in, serve),
            ("history", history_in, history),
            ("push", push_in, push),
            ("features", features_in, features),
            ("mask_in", mask_in_in, mask_in),
            ("mask_out", mask_out_in, mask_out),
            ("initial", initial_in, initial),
            ("weight", weight_in, weight),
            ("cotangent", cotangent_in, cotangent),
        )
    ):
        loads[name] = pltpu.make_async_copy(src, dst, load_sem.at[i])
        if name in ("serve", "history"):
            loads[name].start()

    loads["serve"].wait()
    loads["history"].wait()
    for name in loads:
        if name not in ("serve", "history"):
            loads[name].start()

    def gather(j):
        wanted = serve[:, pl.ds(pl.multiple_of(j * k, 128), k)]
        wanted = jnp.transpose(jnp.broadcast_to(wanted, (128, k)))
        lane = lax.broadcasted_iota(jnp.int32, (k, 128), 1)
        found = dot(
            jnp.concatenate(
                [
                    jnp.where(wanted == lane + 128 * i, 1.0, 0.0).astype(BF16)
                    for i in range(rows // 128)
                ],
                axis=1,
            ),
            history[...],
        )
        return found.astype(BF16)

    for off in range(1, members):
        j = (m + off) % members
        served[off - 1] = gather(j)

    pl.semaphore_wait(barrier, len(near) + beside)
    pulls = []
    for off in range(1, members):
        j = (m + off) % members
        copy = pltpu.make_async_remote_copy(
            src_ref=served.at[off - 1],
            dst_ref=pulled.at[off - 1],
            send_sem=pull_send.at[off - 1],
            recv_sem=pull_recv.at[off - 1],
            device_id=(g, j),
            device_id_type=MESH,
        )
        copy.start()
        pulls.append(copy)
    for di in range(1, low):
        signal(corner_sem, shifted(di, 0))
    if chained:
        along((line_sem.at[0, 0], line_sem.at[0, 1]))

    own = gather(m)
    loads["features"].wait()
    loads["mask_in"].wait()
    loads["mask_out"].wait()
    loads["initial"].wait()

    def columns(j, rows_at):
        return (
            mask_out[rows_at, pl.ds(pl.multiple_of(j * k, 128), k)]
            .astype(F32)
            .astype(BF16)
        )

    for at in blocks:
        summed = features[at, :].astype(F32)
        summed = summed + dot(mask_in[at, :].astype(F32).astype(BF16), features[...])
        summed = summed + dot(columns(m, at), own)
        degree = 1.0 + jnp.sum(
            (mask_in[at, :] + mask_out[at, :]).astype(F32), axis=1, keepdims=True
        )
        share = jnp.broadcast_to((1.0 - ALPHA) / degree, (block, width))
        scale[at, :] = share
        known[at, :] = share * summed + ALPHA * initial[at, :].astype(F32)
        for off in range(1, members):
            others[off - 1, at, :] = columns((m - off + members) % members, at)

    loads["weight"].wait()
    loads["cotangent"].wait()
    if chained:
        heard((line_sem.at[0, 0], line_sem.at[0, 1]))
        along((line_sem.at[1, 0], line_sem.at[1, 1]))

    for copy in pulls:
        copy.wait_recv()
    partial = None
    for at in blocks:
        extra = dot(others[0, at, :], pulled[0])
        for off in range(2, members):
            extra = extra + dot(others[off - 1, at, :], pulled[off - 1])
        support = (known[at, :] + scale[at, :] * extra).astype(BF16)
        mixed = (1.0 - BETA) * support.astype(F32) + BETA * dot(support, weight[...])
        sigma = 0.5 + 0.5 * jnp.tanh(0.5 * mixed)
        embedded[at, :] = (mixed * sigma).astype(BF16)
        delta = (
            cotangent[at, :].astype(F32) * sigma * (1.0 + mixed * (1.0 - sigma))
        ).astype(BF16)
        term = dot(support, delta, ((0,), (0,)))
        partial = term if partial is None else partial + term
    part[...] = (factor * partial).astype(part.dtype)
    if low > 1:
        pl.semaphore_wait(corner_sem, low - 1)

    sends = []
    for i, (di, dm) in enumerate(offsets):
        p = (inner + di) % low * members + (m + dm) % members
        copy = pltpu.make_async_remote_copy(
            src_ref=part.at[pl.ds(pl.multiple_of(p * depth, depth), depth)],
            dst_ref=parts.at[i],
            send_sem=part_send.at[i],
            recv_sem=part_recv.at[i],
            device_id=shifted(di, dm),
            device_id_type=MESH,
        )
        copy.start()
        sends.append(copy)

    loads["push"].wait()

    def hot(j):
        targets = push[:, pl.ds(pl.multiple_of(j * q, 128), q)]
        row = lax.broadcasted_iota(jnp.int32, (rows, q), 0)
        return jnp.where(row == targets, 1.0, 0.0).astype(BF16)

    covered = dot(hot(0), jnp.ones((q, 128), BF16))
    for j in range(1, members):
        covered = covered + dot(hot(j), jnp.ones((q, 128), BF16))
    covered = jnp.concatenate([covered] * (width // 128), axis=1)
    base[...] = jnp.where(covered > 0.5, 0.0, history[...].astype(F32)) + dot(
        hot(m), embedded[pl.ds(pl.multiple_of(m * q, q), q), :]
    )

    mine = part[pl.ds(pl.multiple_of(spot * depth, depth), depth), :].astype(F32)
    for off in range(1, plane):
        sends[off - 1].wait_recv()
        mine = mine + parts[off - 1].astype(F32)
    chunk[...] = mine.astype(chunk.dtype)
    chunks[high] = chunk[...]
    if chained:
        heard((line_sem.at[1, 0], line_sem.at[1, 1]))
    rounds = []
    for off in range(1, planes):
        h = (high + off) % planes
        copy = pltpu.make_async_remote_copy(
            src_ref=chunk,
            dst_ref=chunks.at[high],
            send_sem=chunk_send.at[off - 1],
            recv_sem=chunk_recv.at[off - 1],
            device_id=at_plane(h),
            device_id_type=MESH,
        )
        copy.start()
        rounds.append(copy)

    pushes = []
    for off in range(1, members):
        j = (m + off) % members
        copy = pltpu.make_async_remote_copy(
            src_ref=embedded.at[pl.ds(pl.multiple_of(j * q, q), q)],
            dst_ref=pushed.at[off - 1],
            send_sem=push_send.at[off - 1],
            recv_sem=push_recv.at[off - 1],
            device_id=(g, j),
            device_id_type=MESH,
        )
        copy.start()
        pushes.append(copy)

    for copy in rounds:
        copy.wait_recv()
    whole = chunks[0].astype(F32)
    for h in range(1, planes):
        whole = whole + chunks[h].astype(F32)
    final[...] = whole.astype(final.dtype)
    finals[spot] = final[...]
    lasts = []
    for i, (di, dm) in enumerate(offsets):
        copy = pltpu.make_async_remote_copy(
            src_ref=final,
            dst_ref=finals.at[spot],
            send_sem=final_send.at[i],
            recv_sem=final_recv.at[i],
            device_id=shifted(di, dm),
            device_id_type=MESH,
        )
        copy.start()
        lasts.append(copy)
    fresh = base[...]
    for off in range(1, members):
        j = (m - off + members) % members
        pushes[off - 1].wait_recv()
        fresh = fresh + dot(hot(j), pushed[off - 1])
    history_out[...] = fresh.astype(BF16)

    for copy in lasts:
        copy.wait_recv()
    grad_out[...] = finals[...].astype(F32).reshape(width, width)
    for copy in pulls + sends + pushes + rounds + lasts:
        copy.wait_send()


def local(
    groups,
    members,
    features,
    initial,
    weight,
    mask_in,
    mask_out,
    history,
    serve_rows,
    push_rows,
    cotangent,
):
    batch, width = features.shape
    pull = serve_rows.shape[0]
    rows = history.shape[0]
    low = max(1, 8 // members)
    while groups % low:
        low -= 1
    plane = low * members
    planes = groups // low
    depth = width // plane
    wire = BF16
    factor = BETA / math.sqrt(groups * members * batch)
    vmem = pltpu.VMEM
    dma = pltpu.SemaphoreType.DMA
    anywhere = pl.BlockSpec(memory_space=pl.ANY)
    return pl.pallas_call(
        functools.partial(kernel, groups, members, low, factor),
        out_shape=(
            pltpu.VMEM((width, width), F32),
            pltpu.VMEM((rows, width), BF16),
        ),
        in_specs=[anywhere] * 9,
        out_specs=(pl.BlockSpec(memory_space=pltpu.VMEM),)*2,
        scratch_shapes=[
            vmem(features.shape, BF16),
            vmem(initial.shape, BF16),
            vmem(weight.shape, BF16),
            vmem(mask_in.shape, jnp.int32),
            vmem(mask_out.shape, jnp.int32),
            vmem(history.shape, BF16),
            vmem((1, pull), jnp.int32),
            vmem((1, batch), jnp.int32),
            vmem(cotangent.shape, BF16),
            vmem((members - 1, pull // members, width), BF16),
            vmem((members - 1, pull // members, width), BF16),
            vmem((batch, width), BF16),
            vmem((members - 1, batch // members, width), BF16),
            vmem((rows, width), F32),
            vmem((batch, width), F32),
            vmem((batch, width), F32),
            vmem((members - 1, batch, pull // members), BF16),
            vmem((width, width), wire),
            vmem((plane - 1, depth, width), wire),
            vmem((depth, width), wire),
            vmem((planes, depth, width), wire),
            vmem((depth, width), wire),
            vmem((plane, depth, width), wire),
            dma((9,)),
            pltpu.SemaphoreType.REGULAR,
            pltpu.SemaphoreType.REGULAR((2, 2)),
            dma((members - 1,)),
            dma((members - 1,)),
            dma((members - 1,)),
            dma((members - 1,)),
            dma((plane - 1,)),
            dma((plane - 1,)),
            dma((planes - 1,)),
            dma((planes - 1,)),
            dma((plane - 1,)),
            dma((plane - 1,)),
        ],
        compiler_params=pltpu.CompilerParams(
            collective_id=0, has_side_effects=True, vmem_limit_bytes=62 * 1024 * 1024
        ),
    )(
        features,
        initial,
        weight,
        mask_in,
        mask_out,
        history,
        serve_rows.reshape(1, pull),
        push_rows.reshape(1, batch),
        cotangent,
    )


def solution(mesh):
    groups = mesh.shape["grp"]
    members = mesh.shape["mem"]
    split = P(("grp", "mem"), None)
    return jax.shard_map(
        functools.partial(local, groups, members),
        mesh=mesh,
        in_specs=(split, split, P(), split, split, split, P(("grp", "mem")), P(("grp", "mem")), split),
        out_specs=(P(), split),
        check_vma=False,
    )
```
